256 devices in a mesh: blk: 64 (over z, y_lo, x), win: 4 (over y_hi, core).
Axes of the slice: x: 4, y: 4 (y_hi: 2, y_lo: 2; y = y_hi * 2 + y_lo), z: 8, core: 2. Of those that a mesh axis runs over, the one named last changes fastest.
Arguments:
- raw_traces: bfloat16 [64, 1024, 8192], P('win', None, 'blk'), may hold values from -45 to 45, as said below
- channel_mask: int32 [64, 8192], P('win', 'blk'), may hold values 0 or 1
Outputs:
- cross_first: bfloat16 [256, 2, 8192, 128], P('win', None, 'blk')
- cross_second: bfloat16 [256, 2, 8192, 128], P('win', None, 'blk')
The draws below stay inside these ranges and needn't reach their ends.
Inputs may be any that keep to these rules, and one draw needn't show every extreme that they name: `raw_traces`: each channel has its own gain and each window its own level; all channels share part of the wavefield.
All inputs are finite; a program needn't handle non-finite values. No bound on the sum of `channel_mask` on one device may be relied on, other than what follows from the above.
Results may differ from the reference program's by a relative error of at most 0.0051.
Values may be sent and summed in bfloat16 or wider, within the bound.
No kernel may reach another device: no remote copies, remote signals or barrier semaphores. Data moves between devices by JAX's collectives and lax.ppermute only.
A program may use at most 128 MiB of HBM per device.

```python
import math
import jax
import jax.numpy as jnp
from jax import lax

CH = 128
BINS = 256
SAMPLES = 1024
LOW = 32
BAND = 64
WINDOWS = 64
CHANNELS = 8192
N_BLK = 64


def draw_raw_traces(key, part):
    noise_key = jax.random.fold_in(key, 11)
    common_key = jax.random.fold_in(key, 12)
    channel_key = jax.random.fold_in(key, 13)
    window_key = jax.random.fold_in(key, 14)
    noise_field = jnp.clip(jax.random.normal(noise_key, (WINDOWS, SAMPLES, CHANNELS), jnp.float32), -5.0, 5.0)
    strength = 0.5
    common_field = jnp.clip(jax.random.normal(common_key, (WINDOWS, SAMPLES, 1), jnp.float32), -5.0, 5.0)
    channel_gain = jnp.exp(jax.random.uniform(channel_key, (1, 1, CHANNELS), jnp.float32, math.log(0.3), math.log(3.0)))
    window_gain = jnp.exp(jax.random.uniform(window_key, (WINDOWS, 1, 1), jnp.float32, math.log(0.5), math.log(2.0)))
    return (channel_gain * window_gain * (noise_field + strength * common_field)).astype(jnp.bfloat16)


def place_ends(entries, key, least, top_value):
    index_at = [jax.random.randint(jax.random.fold_in(key, axis), (), 0, length) for axis, length in enumerate(entries.shape)]
    longest = entries.shape.index(max(entries.shape))
    beside = index_at[:longest] + [(index_at[longest] + 1) % entries.shape[longest]] + index_at[longest + 1:]
    return entries.at[tuple(index_at)].set(least).at[tuple(beside)].set(top_value)


def setup_inputs(seed: int = 0) -> dict:
    streams_of = jax.random.split(jax.random.key(seed), 3)
    return {
        "raw_traces": draw_raw_traces(jax.random.fold_in(streams_of[2], 71), 0),
        "channel_mask": place_ends((jax.random.randint(streams_of[1], (WINDOWS, CHANNELS), 0, 8) < 7).astype(jnp.int32), jax.random.fold_in(streams_of[1], 1), 0, 1),
    }


def make_twiddles():
    sample_index = jnp.arange(SAMPLES, dtype=jnp.int32)
    bin_index = LOW + jnp.arange(BINS, dtype=jnp.int32)
    phase_step = sample_index[:, None] * bin_index[None, :] % SAMPLES
    angles = phase_step.astype(jnp.float32) * (2.0 * math.pi / SAMPLES)
    return jnp.stack([jnp.cos(angles), -jnp.sin(angles)], axis=1).astype(jnp.bfloat16)

def whiten_block(traces, mask_rows, twiddles):
    spectra = jnp.einsum('wtc,tkf->wkfc', traces.astype(jnp.float32), twiddles.astype(jnp.float32))
    power_sum = spectra[:, 0] * spectra[:, 0] + spectra[:, 1] * spectra[:, 1]
    window_count = power_sum.shape[0]
    band_power = lax.optimization_barrier(jnp.mean(power_sum.reshape(window_count, BINS // BAND, BAND, power_sum.shape[2]), axis=2))
    band_scale = jnp.repeat(lax.rsqrt(band_power + 1e-06), BAND, axis=1)
    weights = band_scale * mask_rows.astype(jnp.float32)[:, None, :]
    return (spectra * weights[:, None]).astype(jnp.bfloat16)

def cross_block(own_bins, other_bins):
    products = jnp.einsum('wkfi,wlfj->fkilj', own_bins.astype(jnp.float32), other_bins.astype(jnp.float32))
    real_part = products[:, 0, :, 0, :] + products[:, 1, :, 1, :]
    imag_part = products[:, 1, :, 0, :] - products[:, 0, :, 1, :]
    stacked = jnp.stack([real_part, imag_part], axis=1) * (1.0 / math.sqrt(own_bins.shape[0]))
    return stacked.astype(jnp.bfloat16)

def reference(raw_traces, channel_mask):
    twiddles = make_twiddles()
    blocks = raw_traces.reshape(WINDOWS, SAMPLES, N_BLK, CH).transpose(2, 0, 1, 3)
    mask_blocks = channel_mask.reshape(WINDOWS, N_BLK, CH).transpose(1, 0, 2)
    whitened = lax.map(lambda pieces: whiten_block(pieces[0], pieces[1], twiddles), (blocks, mask_blocks))
    bit_count = N_BLK.bit_length() - 1
    outputs = []
    for round_bit in (bit_count - 1, 0):

        def one_block(block_index, round_bit=round_bit):
            partner = jnp.bitwise_xor(block_index, 2 ** round_bit)
            return cross_block(whitened[block_index], whitened[partner])
        block_tiles = lax.map(one_block, jnp.arange(N_BLK, dtype=jnp.int32))
        outputs.append(block_tiles.transpose(1, 2, 0, 3, 4).reshape(BINS, 2, CHANNELS, CH))
    return (outputs[0], outputs[1])
```

```python
import functools
import math

import jax
import jax.numpy as jnp
import ml_dtypes
import numpy as np
from jax import lax
from jax.experimental import pallas as pl
from jax.experimental.pallas import tpu as pltpu
from jax.sharding import PartitionSpec as P

BINS = 256
SAMPLES = 1024
LOW = 32
BAND = 64
BANDS = BINS // BAND
CH = 128
WINS = 16
PAIR = 2
VMEM_LIMIT = 40 * 1024 * 1024


def band_twiddles():
    sample_index = np.arange(SAMPLES, dtype=np.int32)
    bin_index = LOW + np.arange(BINS, dtype=np.int32)
    phase_step = bin_index[:, None] * sample_index[None, :] % SAMPLES
    angles = phase_step.astype(np.float32) * np.float32(2.0 * math.pi / SAMPLES)
    table = np.stack(
        [np.cos(angles).reshape(BANDS, BAND, SAMPLES), -np.sin(angles).reshape(BANDS, BAND, SAMPLES)],
        axis=1,
    )
    return table.reshape(BANDS, 2 * BAND, SAMPLES).astype(ml_dtypes.bfloat16)


def spectra_kernel(parts, band_ref, *refs):
    twiddle_refs = refs[:parts]
    raw_ref, mask_ref = refs[parts], refs[parts + 1]
    out_refs = refs[parts + 2 : 2 * parts + 2]
    wide_refs = refs[2 * parts + 2 :]
    step = pl.program_id(0)
    pair = jnp.concatenate([raw_ref[0], raw_ref[1]], axis=1)
    for part in range(parts):
        spectra = jnp.dot(twiddle_refs[part][0], pair, preferred_element_type=jnp.float32)
        real, imag = spectra[:BAND], spectra[BAND:]
        power = jnp.sum(real * real + imag * imag, axis=0, keepdims=True) * (1.0 / BAND)
        scale = lax.rsqrt(power + 1e-06)
        for half in range(PAIR):
            window = step * PAIR + half
            cols = slice(half * CH, (half + 1) * CH)
            weight = scale[:, cols] * mask_ref[pl.ds(window, 1), :].astype(jnp.float32)
            wide_refs[part][pl.ds(window, BAND, stride=2 * WINS), :] = real[:, cols] * weight
            wide_refs[part][pl.ds(window + WINS, BAND, stride=2 * WINS), :] = imag[:, cols] * weight

    @pl.when(step == pl.num_programs(0) - 1)
    def _():
        for part in range(parts):
            out_refs[part][...] = wide_refs[part][...].astype(jnp.bfloat16)


def whiten_bands(bands, table, raw_traces, channel_mask):
    parts = bands.shape[0]

    def band_spec(part):
        return pl.BlockSpec((1, 2 * BAND, SAMPLES), lambda step, band_ref: (band_ref[part], 0, 0))

    rows = BAND * 2 * WINS
    return pl.pallas_call(
        functools.partial(spectra_kernel, parts),
        out_shape=[jax.ShapeDtypeStruct((rows, CH), jnp.bfloat16)] * parts,
        grid_spec=pltpu.PrefetchScalarGridSpec(
            num_scalar_prefetch=1,
            grid=(WINS // PAIR,),
            in_specs=[band_spec(part) for part in range(parts)]
            + [
                pl.BlockSpec((PAIR, SAMPLES, CH), lambda step, band_ref: (step, 0, 0)),
                pl.BlockSpec((WINS, CH), lambda step, band_ref: (0, 0)),
            ],
            out_specs=[pl.BlockSpec((rows, CH), lambda step, band_ref: (0, 0))] * parts,
            scratch_shapes=[pltpu.VMEM((rows, CH), jnp.float32)] * parts,
        ),
        compiler_params=pltpu.CompilerParams(vmem_limit_bytes=VMEM_LIMIT),
        cost_estimate=pl.CostEstimate(
            flops=2 * WINS * CH * SAMPLES * 2 * BAND * parts,
            bytes_accessed=2 * WINS * CH * SAMPLES + parts * 2 * rows * CH,
            transcendentals=0,
        ),
    )(bands, *([table] * parts), raw_traces, channel_mask)


def cross_kernel(count, bins, *refs):
    own_refs, other_refs, out_ref = refs[:BANDS], refs[BANDS : 2 * BANDS], refs[2 * BANDS]
    scale = 1.0 / math.sqrt(WINS * BANDS)
    for index in range(bins):
        rows = slice(index * 2 * WINS, (index + 1) * 2 * WINS)
        own = [ref[rows, :] for ref in own_refs]
        turned = []
        for piece in own:
            turned += [piece[WINS:], -piece[:WINS]]
        left = jnp.concatenate([jnp.concatenate(own, axis=0), jnp.concatenate(turned, axis=0)], axis=1)
        right = jnp.concatenate([ref[rows, :] for ref in other_refs], axis=0)
        tile = lax.dot_general(left, right, (((0,), (0,)), ((), ())), preferred_element_type=jnp.float32)
        tile = (tile * scale).astype(jnp.bfloat16)
        out_ref[index, 0] = tile[:CH]
        out_ref[index, 1] = tile[CH:]


def cross_blocks(own, other):
    bins = 8
    rows = bins * 2 * WINS
    piece = pl.BlockSpec((rows, CH), lambda step: (step, 0))
    return pl.pallas_call(
        functools.partial(cross_kernel, WINS * BANDS, bins),
        out_shape=jax.ShapeDtypeStruct((BAND, 2, CH, CH), jnp.bfloat16),
        grid=(BAND // bins,),
        in_specs=[piece] * (2 * BANDS),
        out_specs=pl.BlockSpec((bins, 2, CH, CH), lambda step: (step, 0, 0, 0)),
        compiler_params=pltpu.CompilerParams(vmem_limit_bytes=VMEM_LIMIT),
        cost_estimate=pl.CostEstimate(
            flops=2 * BAND * 2 * CH * CH * 2 * WINS * BANDS,
            bytes_accessed=2 * BAND * 2 * CH * CH + 4 * BANDS * BAND * 2 * WINS * CH,
            transcendentals=0,
        ),
    )(*own, *other)


def swap_win(piece, offset):
    return lax.ppermute(piece, "win", [(i, i ^ offset) for i in range(lax.axis_size("win"))])


def swap_blk(piece, stride):
    return lax.ppermute(piece, "blk", [(i, i ^ stride) for i in range(lax.axis_size("blk"))])


def body(raw_traces, channel_mask):
    table = jnp.asarray(band_twiddles())
    mine = lax.axis_index("win").astype(jnp.int32)
    (own_piece,) = whiten_bands(mine[None], table, raw_traces, channel_mask)
    others = jnp.stack([mine ^ offset for offset in range(1, BANDS)])
    leaving = whiten_bands(others, table, raw_traces, channel_mask)
    own = [own_piece] + [swap_win(leaving[offset - 1], offset) for offset in range(1, BANDS)]
    far = lax.axis_size("blk") // 2
    results = []
    for stride in (far, 1):
        other = [swap_blk(piece, stride) for piece in own]
        results.append(cross_blocks(own, other))
    return tuple(results)


def solution(mesh):
    in_specs = (P("win", None, "blk"), P("win", "blk"))
    out_specs = (P("win", None, "blk", None), P("win", None, "blk", None))
    return jax.shard_map(body, mesh=mesh, in_specs=in_specs, out_specs=out_specs, check_vma=False)
```

```python
import functools
import math

import jax
import jax.numpy as jnp
import ml_dtypes
import numpy as np
from jax import lax
from jax.experimental import pallas as pl
from jax.experimental.pallas import tpu as pltpu
from jax.sharding import PartitionSpec as P

BINS = 256
SAMPLES = 1024
LOW = 32
BAND = 64
BANDS = BINS // BAND
CH = 128
WINS = 16
ROWS = 2 * WINS
PITCH = 40
PAIR = 2
GROUP = 8
STEP = 8
HEAD = 48
VMEM_LIMIT = 48 * 1024 * 1024
SPECTRA_VMEM = 62 * 1024 * 1024


def band_twiddles():
    sample_index = np.arange(SAMPLES, dtype=np.int32)
    bin_index = LOW + np.arange(BINS, dtype=np.int32)
    phase_step = bin_index[:, None] * sample_index[None, :] % SAMPLES
    angles = phase_step.astype(np.float32) * np.float32(2.0 * math.pi / SAMPLES)
    table = np.stack(
        [np.cos(angles).reshape(BANDS, BAND, SAMPLES), -np.sin(angles).reshape(BANDS, BAND, SAMPLES)],
        axis=1,
    )
    return table.reshape(BANDS, 2 * BAND, SAMPLES).astype(ml_dtypes.bfloat16)


def spectra_kernel(offsets, outs, table_ref, raw_ref, mask_ref, *refs):
    parts = len(offsets)
    out_refs, refs = refs[: len(outs)], refs[len(outs) :]
    twiddle, raw, mask = refs[:3]
    wide_refs = refs[3 : parts + 3]
    twiddle_sems, raw_sems, mask_sem = refs[parts + 3 :]
    mine = lax.axis_index("win")
    mask_copy = pltpu.make_async_copy(mask_ref, mask, mask_sem)
    twiddle_copies = [
        pltpu.make_async_copy(
            table_ref.at[lax.bitwise_xor(mine, jnp.int32(offset))], twiddle.at[part], twiddle_sems.at[part]
        )
        for part, offset in enumerate(offsets)
    ]
    raw_copies = [
        pltpu.make_async_copy(
            raw_ref.at[pl.ds(group * GROUP, GROUP)], raw.at[pl.ds(group * GROUP, GROUP)], raw_sems.at[group]
        )
        for group in range(WINS // GROUP)
    ]
    for copy in [mask_copy] + twiddle_copies + raw_copies:
        copy.start()
    for copy in [mask_copy] + twiddle_copies:
        copy.wait()
    left = twiddle[...].reshape(parts * 2 * BAND, SAMPLES)
    for group in range(WINS // GROUP):
        raw_copies[group].wait()
        for first in range(group * GROUP, (group + 1) * GROUP, PAIR):
            pair = jnp.concatenate([raw[first], raw[first + 1]], axis=1)
            spectra = jnp.dot(left, pair, preferred_element_type=jnp.float32)
            for part in range(parts):
                real = spectra[part * 2 * BAND : (part * 2 + 1) * BAND]
                imag = spectra[(part * 2 + 1) * BAND : (part * 2 + 2) * BAND]
                power = jnp.sum(real * real + imag * imag, axis=0, keepdims=True) * (1.0 / BAND)
                scale = lax.rsqrt(power + 1e-06)
                for half in range(PAIR):
                    window = first + half
                    cols = slice(half * CH, (half + 1) * CH)
                    weight = scale[:, cols] * mask[window : window + 1, :].astype(jnp.float32)
                    wide = wide_refs[part]
                    wide[pl.ds(window, BAND, stride=PITCH), :] = real[:, cols] * weight
                    wide[pl.ds(window + WINS, BAND, stride=PITCH), :] = imag[:, cols] * weight
    for out_ref, (part, start, stop) in zip(out_refs, outs):
        for bin_index in range(start, stop):
            out_ref[(bin_index - start) * ROWS : (bin_index - start + 1) * ROWS, :] = wide_refs[part][
                bin_index * PITCH : bin_index * PITCH + ROWS, :
            ].astype(jnp.bfloat16)


def whiten_bands(offsets, outs, table, raw_traces, channel_mask):
    parts = len(offsets)
    anywhere = pl.BlockSpec(memory_space=pltpu.HBM)
    return pl.pallas_call(
        functools.partial(spectra_kernel, offsets, outs),
        out_shape=[
            jax.ShapeDtypeStruct(((stop - start) * ROWS, CH), jnp.bfloat16) for _, start, stop in outs
        ],
        in_specs=[anywhere] * 3,
        out_specs=[pl.BlockSpec(memory_space=pltpu.VMEM)] * len(outs),
        scratch_shapes=[
            pltpu.VMEM((parts, 2 * BAND, SAMPLES), jnp.bfloat16),
            pltpu.VMEM((WINS, SAMPLES, CH), jnp.bfloat16),
            pltpu.VMEM((WINS, CH), jnp.int32),
        ]
        + [pltpu.VMEM((BAND * PITCH, CH), jnp.float32)] * parts
        + [
            pltpu.SemaphoreType.DMA((parts,)),
            pltpu.SemaphoreType.DMA((WINS // GROUP,)),
            pltpu.SemaphoreType.DMA(()),
        ],
        compiler_params=pltpu.CompilerParams(vmem_limit_bytes=SPECTRA_VMEM),
        cost_estimate=pl.CostEstimate(
            flops=2 * WINS * CH * SAMPLES * 2 * BAND * parts,
            bytes_accessed=2 * WINS * CH * SAMPLES + parts * 2 * BAND * ROWS * CH,
            transcendentals=0,
        ),
    )(table, raw_traces, channel_mask)


def cross_kernel(bins, *refs):
    own_refs, other_refs, out_ref = refs[:BANDS], refs[BANDS : 2 * BANDS], refs[-1]
    scale = 1.0 / math.sqrt(WINS * BANDS)
    for index in range(bins):
        rows = slice(index * ROWS, (index + 1) * ROWS)
        own = [ref[rows, :] for ref in own_refs]
        turned = []
        for piece in own:
            turned += [piece[WINS:], -piece[:WINS]]
        left = jnp.concatenate([jnp.concatenate(own, axis=0), jnp.concatenate(turned, axis=0)], axis=1)
        right = jnp.concatenate([ref[rows, :] for ref in other_refs], axis=0)
        tile = lax.dot_general(left, right, (((0,), (0,)), ((), ())), preferred_element_type=jnp.float32)
        tile = (tile * scale).astype(jnp.bfloat16)
        out_ref[index, 0] = tile[:CH]
        out_ref[index, 1] = tile[CH:]


def cross_blocks(own, other, first, last, into=None):
    bins = STEP
    steps = (last - first) // bins

    def piece(start):
        return pl.BlockSpec((bins * ROWS, CH), lambda step: ((first - start) // bins + step, 0))

    arrays = list(own) + [array for array, _ in other]
    in_specs = [piece(0)] * BANDS + [piece(start) for _, start in other]
    aliases = {}
    if into is not None:
        aliases = {len(arrays): 0}
        arrays.append(into)
        in_specs.append(pl.BlockSpec(memory_space=pl.ANY))
    return pl.pallas_call(
        functools.partial(cross_kernel, bins),
        out_shape=jax.ShapeDtypeStruct((BAND, 2, CH, CH), jnp.bfloat16),
        grid=(steps,),
        in_specs=in_specs,
        out_specs=pl.BlockSpec((bins, 2, CH, CH), lambda step: (first // bins + step, 0, 0, 0)),
        input_output_aliases=aliases,
        compiler_params=pltpu.CompilerParams(vmem_limit_bytes=VMEM_LIMIT),
        cost_estimate=pl.CostEstimate(
            flops=2 * (last - first) * 2 * CH * CH * 2 * WINS * BANDS,
            bytes_accessed=(last - first) * (4 * CH * CH + 4 * BANDS * ROWS * CH),
            transcendentals=0,
        ),
    )(*arrays)


def swap_win(piece, offset):
    return lax.ppermute(piece, "win", [(i, i ^ offset) for i in range(lax.axis_size("win"))])


def swap_blk(piece, stride):
    return lax.ppermute(piece, "blk", [(i, i ^ stride) for i in range(lax.axis_size("blk"))])


def tie(*arrays):
    return lax.optimization_barrier(arrays)


def body(raw_traces, channel_mask):
    table = jnp.asarray(band_twiddles())
    far = lax.axis_size("blk") // 2
    split = HEAD * ROWS
    pieces = tuple((part, 0, BAND) for part in range(BANDS))
    own0, leaving1, leaving2, leaving3 = whiten_bands(tuple(range(BANDS)), pieces, table, raw_traces, channel_mask)
    far0 = swap_blk(own0, far)
    own3, own2, own1 = swap_win(leaving3, 3), swap_win(leaving2, 2), swap_win(leaving1, 1)
    head = jnp.concatenate([own2[:split], own3[:split]])
    tail = jnp.concatenate([own2[split:], own3[split:]])
    near0 = swap_blk(own0, 1)
    far1 = swap_blk(own1, far)
    own1_next, far0, near0 = tie(own1, far0, near0)
    near1 = swap_blk(own1_next, 1)
    near23 = swap_blk(jnp.concatenate([own2, own3]), 1)
    far_head, far_tail = swap_blk(head, far), swap_blk(tail, far)
    own = (own0, own1, own2, own3)
    far_pieces = [(far0, 0), (far1, 0)]
    second = cross_blocks(own, [(near0, 0), (near1, 0), (near23, 0), (near23, -BAND)], 0, BAND)
    far_head, second = tie(far_head, second)
    first = cross_blocks(own, far_pieces + [(far_head, 0), (far_head, -HEAD)], 0, HEAD)
    first = cross_blocks(own, far_pieces + [(far_tail, HEAD), (far_tail, 2 * HEAD - BAND)], HEAD, BAND, first)
    return first, second


def solution(mesh):
    in_specs = (P("win", None, "blk"), P("win", "blk"))
    out_specs = (P("win", None, "blk", None), P("win", None, "blk", None))
    return jax.shard_map(body, mesh=mesh, in_specs=in_specs, out_specs=out_specs, check_vma=False)
```

```python
import functools
import math

import jax
import jax.numpy as jnp
import ml_dtypes
import numpy as np
from jax import lax
from jax.experimental import pallas as pl
from jax.experimental.pallas import tpu as pltpu
from jax.sharding import PartitionSpec as P

BINS = 256
SAMPLES = 1024
LOW = 32
BAND = 64
BANDS = BINS // BAND
CH = 128
WINS = 16
ROWS = 2 * WINS
PITCH = 40
PAIR = 2
GROUP = 8
CHUNK = 8
VMEM_LIMIT = 32 * 1024 * 1024
SPECTRA_VMEM = 62 * 1024 * 1024


def band_twiddles():
    sample_index = np.arange(SAMPLES, dtype=np.int32)
    bin_index = LOW + np.arange(BINS, dtype=np.int32)
    phase_step = bin_index[:, None] * sample_index[None, :] % SAMPLES
    angles = phase_step.astype(np.float32) * np.float32(2.0 * math.pi / SAMPLES)
    table = np.stack(
        [np.cos(angles).reshape(BANDS, BAND, SAMPLES), -np.sin(angles).reshape(BANDS, BAND, SAMPLES)],
        axis=1,
    )
    return table.reshape(BANDS, 2 * BAND, SAMPLES).astype(ml_dtypes.bfloat16)


def spectra_kernel(offsets, outs, table_ref, raw_ref, mask_ref, *refs):
    parts = len(offsets)
    out_refs, refs = refs[: len(outs)], refs[len(outs) :]
    twiddle, raw, mask = refs[:3]
    wide_refs = refs[3 : parts + 3]
    twiddle_sems, raw_sems, mask_sem = refs[parts + 3 :]
    mine = lax.axis_index("win")
    mask_copy = pltpu.make_async_copy(mask_ref, mask, mask_sem)
    twiddle_copies = [
        pltpu.make_async_copy(
            table_ref.at[lax.bitwise_xor(mine, jnp.int32(offset))], twiddle.at[part], twiddle_sems.at[part]
        )
        for part, offset in enumerate(offsets)
    ]
    raw_copies = [
        pltpu.make_async_copy(
            raw_ref.at[pl.ds(group * GROUP, GROUP)], raw.at[pl.ds(group * GROUP, GROUP)], raw_sems.at[group]
        )
        for group in range(WINS // GROUP)
    ]
    for copy in [mask_copy] + twiddle_copies + raw_copies:
        copy.start()
    for copy in [mask_copy] + twiddle_copies:
        copy.wait()
    left = twiddle[...].reshape(parts * 2 * BAND, SAMPLES)
    for group in range(WINS // GROUP):
        raw_copies[group].wait()
        for first in range(group * GROUP, (group + 1) * GROUP, PAIR):
            pair = jnp.concatenate([raw[first], raw[first + 1]], axis=1)
            spectra = jnp.dot(left, pair, preferred_element_type=jnp.float32)
            for part in range(parts):
                real = spectra[part * 2 * BAND : (part * 2 + 1) * BAND]
                imag = spectra[(part * 2 + 1) * BAND : (part * 2 + 2) * BAND]
                power = jnp.sum(real * real + imag * imag, axis=0, keepdims=True) * (1.0 / BAND)
                scale = lax.rsqrt(power + 1e-06)
                for half in range(PAIR):
                    window = first + half
                    cols = slice(half * CH, (half + 1) * CH)
                    weight = scale[:, cols] * mask[window : window + 1, :].astype(jnp.float32)
                    wide = wide_refs[part]
                    wide[pl.ds(window, BAND, stride=PITCH), :] = real[:, cols] * weight
                    wide[pl.ds(window + WINS, BAND, stride=PITCH), :] = imag[:, cols] * weight
    for out_ref, runs in zip(out_refs, outs):
        for place, part in enumerate(runs):
            for bin_index in range(BAND):
                row = (place * BAND + bin_index) * ROWS
                out_ref[row : row + ROWS, :] = wide_refs[part][
                    bin_index * PITCH : bin_index * PITCH + ROWS, :
                ].astype(jnp.bfloat16)


def whiten_bands(offsets, outs, table, raw_traces, channel_mask):
    parts = len(offsets)
    anywhere = pl.BlockSpec(memory_space=pltpu.HBM)
    return pl.pallas_call(
        functools.partial(spectra_kernel, offsets, outs),
        out_shape=[
            jax.ShapeDtypeStruct((len(runs) * BAND * ROWS, CH), jnp.bfloat16) for runs in outs
        ],
        in_specs=[anywhere] * 3,
        out_specs=[pl.BlockSpec(memory_space=pltpu.VMEM)] * len(outs),
        scratch_shapes=[
            pltpu.VMEM((parts, 2 * BAND, SAMPLES), jnp.bfloat16),
            pltpu.VMEM((WINS, SAMPLES, CH), jnp.bfloat16),
            pltpu.VMEM((WINS, CH), jnp.int32),
        ]
        + [pltpu.VMEM((BAND * PITCH, CH), jnp.float32)] * parts
        + [
            pltpu.SemaphoreType.DMA((parts,)),
            pltpu.SemaphoreType.DMA((WINS // GROUP,)),
            pltpu.SemaphoreType.DMA(()),
        ],
        compiler_params=pltpu.CompilerParams(vmem_limit_bytes=SPECTRA_VMEM),
        cost_estimate=pl.CostEstimate(
            flops=2 * WINS * CH * SAMPLES * 2 * BAND * parts,
            bytes_accessed=2 * WINS * CH * SAMPLES + parts * 2 * BAND * ROWS * CH,
            transcendentals=0,
        ),
    )(table, raw_traces, channel_mask)


def cross_kernel(first, last, starts, *refs):
    count = len(starts)
    piece_refs, out_ref, tiles, sems = refs[:count], refs[-3], refs[-2], refs[-1]
    scale = 1.0 / math.sqrt(WINS * BANDS)

    def copy_out(chunk):
        bins = pl.ds(chunk * CHUNK, CHUNK)
        to = pl.ds(first + chunk * CHUNK, CHUNK)
        return pltpu.make_async_copy(tiles.at[bins], out_ref.at[to], sems.at[chunk])

    @pl.loop(0, (last - first) // CHUNK)
    def _(chunk):
        for index in range(CHUNK):
            bin_index = chunk * CHUNK + index
            pieces = [
                ref[pl.ds(pl.multiple_of((first - start + bin_index) * ROWS, ROWS), ROWS), :]
                for ref, start in zip(piece_refs, starts)
            ]
            own, other = pieces[:BANDS], pieces[BANDS:]
            turned = []
            for piece in own:
                turned += [piece[WINS:], -piece[:WINS]]
            left = jnp.concatenate([jnp.concatenate(own, axis=0), jnp.concatenate(turned, axis=0)], axis=1)
            right = jnp.concatenate(other, axis=0)
            tile = lax.dot_general(left, right, (((0,), (0,)), ((), ())), preferred_element_type=jnp.float32)
            tile = (tile * scale).astype(jnp.bfloat16)
            tiles[bin_index, 0] = tile[:CH]
            tiles[bin_index, 1] = tile[CH:]
        copy_out(chunk).start()

    @pl.loop(0, (last - first) // CHUNK)
    def _(chunk):
        copy_out(chunk).wait()


def cross_blocks(own, other, first, last, into=None):
    arrays = [array for array, _ in own + other]
    starts = tuple(start for _, start in own + other)
    in_specs = [pl.BlockSpec(memory_space=pltpu.VMEM)] * len(arrays)
    aliases = {}
    if into is not None:
        aliases = {len(arrays): 0}
        arrays.append(into)
        in_specs.append(pl.BlockSpec(memory_space=pltpu.HBM))
    return pl.pallas_call(
        functools.partial(cross_kernel, first, last, starts),
        out_shape=jax.ShapeDtypeStruct((BAND, 2, CH, CH), jnp.bfloat16),
        in_specs=in_specs,
        out_specs=pl.BlockSpec(memory_space=pltpu.HBM),
        scratch_shapes=[
            pltpu.VMEM((last - first, 2, CH, CH), jnp.bfloat16),
            pltpu.SemaphoreType.DMA(((last - first) // CHUNK,)),
        ],
        input_output_aliases=aliases,
        compiler_params=pltpu.CompilerParams(vmem_limit_bytes=VMEM_LIMIT),
        cost_estimate=pl.CostEstimate(
            flops=2 * (last - first) * 2 * CH * CH * 2 * WINS * BANDS,
            bytes_accessed=(last - first) * (4 * CH * CH + 4 * BANDS * ROWS * CH),
            transcendentals=0,
        ),
    )(*arrays)


def swap(piece, stride, offset):
    blks, wins = lax.axis_size("blk"), lax.axis_size("win")
    route = [
        (blk * wins + win, (blk ^ stride) * wins + (win ^ offset)) for blk in range(blks) for win in range(wins)
    ]
    return lax.ppermute(piece, ("blk", "win"), route)


def swap_blk(piece, stride):
    return swap(piece, stride, 0)


def tie(*arrays):
    return lax.optimization_barrier(arrays)


def body(raw_traces, channel_mask):
    table = jnp.asarray(band_twiddles())
    far = lax.axis_size("blk") // 2
    rows = BAND * ROWS
    own0, leaving2, leaving13 = whiten_bands((0, 1, 2, 3), ((0,), (2,), (1, 3)), table, raw_traces, channel_mask)
    from_core = swap(leaving13, 0, 1)
    own1 = from_core[:rows]
    same = jnp.concatenate([own0, own1])
    cross = jnp.concatenate([leaving2, from_core[rows:]])
    far01 = swap(same, far, 0)
    far23 = swap(cross, far, 2)
    arrived = swap(cross, 0, 2)
    own2, own3 = arrived[:rows], arrived[rows:]
    own0_next, arrived = tie(own0, arrived)
    near0, near1 = swap_blk(own0_next, 1), swap_blk(own1, 1)
    near2, near3 = swap_blk(own2, 1), swap_blk(own3, 1)
    near = [(near0, 0), (near1, 0), (near2, 0), (near3, 0)]
    own = [(same, 0), (same, -BAND), (arrived, 0), (arrived, -BAND)]
    second = cross_blocks(own, near, 0, BAND)
    far01, far23, second = tie(far01, far23, second)
    far_pieces = [(far01, 0), (far01, -BAND), (far23, 0), (far23, -BAND)]
    first = cross_blocks(own, far_pieces, 0, BAND)
    return first, second


def solution(mesh):
    in_specs = (P("win", None, "blk"), P("win", "blk"))
    out_specs = (P("win", None, "blk", None), P("win", None, "blk", None))
    return jax.shard_map(body, mesh=mesh, in_specs=in_specs, out_specs=out_specs, check_vma=False)
```

```python
import functools
import math

import jax
import jax.numpy as jnp
import ml_dtypes
import numpy as np
from jax import lax
from jax.experimental import pallas as pl
from jax.experimental.pallas import tpu as pltpu
from jax.sharding import PartitionSpec as P

BINS = 256
SAMPLES = 1024
LOW = 32
BAND = 64
BANDS = BINS // BAND
CH = 128
WINS = 16
ROWS = 2 * WINS
PITCH = 40
PAIR = 2
GROUP = 8
CHUNK = 8
VMEM_LIMIT = 32 * 1024 * 1024
SPECTRA_VMEM = 62 * 1024 * 1024


def band_twiddles():
    sample_index = np.arange(SAMPLES, dtype=np.int32)
    bin_index = LOW + np.arange(BINS, dtype=np.int32)
    phase_step = bin_index[:, None] * sample_index[None, :] % SAMPLES
    angles = phase_step.astype(np.float32) * np.float32(2.0 * math.pi / SAMPLES)
    table = np.stack(
        [np.cos(angles).reshape(BANDS, BAND, SAMPLES), -np.sin(angles).reshape(BANDS, BAND, SAMPLES)],
        axis=1,
    )
    return table.reshape(BANDS, 2 * BAND, SAMPLES).astype(ml_dtypes.bfloat16)


def spectra_kernel(offsets, outs, table_ref, raw_ref, mask_ref, *refs):
    parts = len(offsets)
    out_refs, refs = refs[: len(outs)], refs[len(outs) :]
    twiddle, raw, mask = refs[:3]
    wide_refs = refs[3 : parts + 3]
    twiddle_sems, raw_sems, mask_sem = refs[parts + 3 :]
    mine = lax.axis_index("win")
    mask_copy = pltpu.make_async_copy(mask_ref, mask, mask_sem)
    twiddle_copies = [
        pltpu.make_async_copy(
            table_ref.at[lax.bitwise_xor(mine, jnp.int32(offset))], twiddle.at[part], twiddle_sems.at[part]
        )
        for part, offset in enumerate(offsets)
    ]
    raw_copies = [
        pltpu.make_async_copy(
            raw_ref.at[pl.ds(group * GROUP, GROUP)], raw.at[pl.ds(group * GROUP, GROUP)], raw_sems.at[group]
        )
        for group in range(WINS // GROUP)
    ]
    for copy in [mask_copy] + twiddle_copies + raw_copies:
        copy.start()
    for copy in [mask_copy] + twiddle_copies:
        copy.wait()
    left = twiddle[...].reshape(parts * 2 * BAND, SAMPLES)
    for group in range(WINS // GROUP):
        raw_copies[group].wait()
        for first in range(group * GROUP, (group + 1) * GROUP, PAIR):
            pair = jnp.concatenate([raw[first], raw[first + 1]], axis=1)
            spectra = jnp.dot(left, pair, preferred_element_type=jnp.float32)
            for part in range(parts):
                real = spectra[part * 2 * BAND : (part * 2 + 1) * BAND]
                imag = spectra[(part * 2 + 1) * BAND : (part * 2 + 2) * BAND]
                power = jnp.sum(real * real + imag * imag, axis=0, keepdims=True) * (1.0 / BAND)
                scale = lax.rsqrt(power + 1e-06)
                for half in range(PAIR):
                    window = first + half
                    cols = slice(half * CH, (half + 1) * CH)
                    weight = scale[:, cols] * mask[window : window + 1, :].astype(jnp.float32)
                    wide = wide_refs[part]
                    wide[pl.ds(window, BAND, stride=PITCH), :] = real[:, cols] * weight
                    wide[pl.ds(window + WINS, BAND, stride=PITCH), :] = imag[:, cols] * weight
    for out_ref, runs in zip(out_refs, outs):
        for place, part in enumerate(runs):
            for bin_index in range(BAND):
                row = (place * BAND + bin_index) * ROWS
                out_ref[row : row + ROWS, :] = wide_refs[part][
                    bin_index * PITCH : bin_index * PITCH + ROWS, :
                ].astype(jnp.bfloat16)


def whiten_bands(offsets, outs, table, raw_traces, channel_mask):
    parts = len(offsets)
    anywhere = pl.BlockSpec(memory_space=pltpu.HBM)
    return pl.pallas_call(
        functools.partial(spectra_kernel, offsets, outs),
        out_shape=[
            jax.ShapeDtypeStruct((len(runs) * BAND * ROWS, CH), jnp.bfloat16) for runs in outs
        ],
        in_specs=[anywhere] * 3,
        out_specs=[pl.BlockSpec(memory_space=pltpu.VMEM)] * len(outs),
        scratch_shapes=[
            pltpu.VMEM((parts, 2 * BAND, SAMPLES), jnp.bfloat16),
            pltpu.VMEM((WINS, SAMPLES, CH), jnp.bfloat16),
            pltpu.VMEM((WINS, CH), jnp.int32),
        ]
        + [pltpu.VMEM((BAND * PITCH, CH), jnp.float32)] * parts
        + [
            pltpu.SemaphoreType.DMA((parts,)),
            pltpu.SemaphoreType.DMA((WINS // GROUP,)),
            pltpu.SemaphoreType.DMA(()),
        ],
        compiler_params=pltpu.CompilerParams(vmem_limit_bytes=SPECTRA_VMEM),
        cost_estimate=pl.CostEstimate(
            flops=2 * WINS * CH * SAMPLES * 2 * BAND * parts,
            bytes_accessed=2 * WINS * CH * SAMPLES + parts * 2 * BAND * ROWS * CH,
            transcendentals=0,
        ),
    )(table, raw_traces, channel_mask)


def cross_kernel(first, last, starts, *refs):
    count = len(starts)
    piece_refs, out_ref, left_ref, tiles, sems = refs[:count], refs[-4], refs[-3], refs[-2], refs[-1]
    if count == BANDS:
        left_ref, out_ref = refs[count], refs[-3]
    scale = 1.0 / math.sqrt(WINS * BANDS)

    def copy_out(chunk):
        bins = pl.ds(chunk * CHUNK, CHUNK)
        to = pl.ds(first + chunk * CHUNK, CHUNK)
        return pltpu.make_async_copy(tiles.at[bins], out_ref.at[to], sems.at[chunk])

    @pl.loop(0, (last - first) // CHUNK)
    def _(chunk):
        for index in range(CHUNK):
            bin_index = chunk * CHUNK + index
            pieces = [
                ref[pl.ds(pl.multiple_of((first - start + bin_index) * ROWS, ROWS), ROWS), :]
                for ref, start in zip(piece_refs, starts)
            ]
            right = jnp.concatenate(pieces[-BANDS:], axis=0)
            if count > BANDS:
                own = pieces[:BANDS]
                turned = []
                for piece in own:
                    turned += [piece[WINS:], -piece[:WINS]]
                left = jnp.concatenate([jnp.concatenate(own, axis=0), jnp.concatenate(turned, axis=0)], axis=1)
                left_ref[bin_index] = left.T
            tile = jnp.dot(left_ref[bin_index], right, preferred_element_type=jnp.float32)
            tile = (tile * scale).astype(jnp.bfloat16)
            tiles[bin_index, 0] = tile[:CH]
            tiles[bin_index, 1] = tile[CH:]
        copy_out(chunk).start()

    @pl.loop(0, (last - first) // CHUNK)
    def _(chunk):
        copy_out(chunk).wait()


def cross_blocks(own, other, first, last, left=None):
    pieces = own + other if left is None else other
    arrays = [array for array, _ in pieces] + ([] if left is None else [left])
    starts = tuple(start for _, start in pieces)
    in_specs = [pl.BlockSpec(memory_space=pltpu.VMEM)] * len(arrays)
    out_shape = [jax.ShapeDtypeStruct((BAND, 2, CH, CH), jnp.bfloat16)]
    out_specs = [pl.BlockSpec(memory_space=pltpu.HBM)]
    if left is None:
        out_shape.append(jax.ShapeDtypeStruct((BAND, 2 * CH, ROWS * BANDS), jnp.bfloat16))
        out_specs.append(pl.BlockSpec(memory_space=pltpu.VMEM))
    return pl.pallas_call(
        functools.partial(cross_kernel, first, last, starts),
        out_shape=out_shape,
        in_specs=in_specs,
        out_specs=out_specs,
        scratch_shapes=[
            pltpu.VMEM((last - first, 2, CH, CH), jnp.bfloat16),
            pltpu.SemaphoreType.DMA(((last - first) // CHUNK,)),
        ],
        compiler_params=pltpu.CompilerParams(vmem_limit_bytes=VMEM_LIMIT),
        cost_estimate=pl.CostEstimate(
            flops=2 * (last - first) * 2 * CH * CH * 2 * WINS * BANDS,
            bytes_accessed=(last - first) * (4 * CH * CH + 4 * BANDS * ROWS * CH),
            transcendentals=0,
        ),
    )(*arrays)


def swap(piece, stride, offset):
    blks, wins = lax.axis_size("blk"), lax.axis_size("win")
    route = [
        (blk * wins + win, (blk ^ stride) * wins + (win ^ offset)) for blk in range(blks) for win in range(wins)
    ]
    return lax.ppermute(piece, ("blk", "win"), route)


def swap_blk(piece, stride):
    return swap(piece, stride, 0)


def tie(*arrays):
    return lax.optimization_barrier(arrays)


def body(raw_traces, channel_mask):
    table = jnp.asarray(band_twiddles())
    far = lax.axis_size("blk") // 2
    rows = BAND * ROWS
    own0, leaving2, leaving13 = whiten_bands((0, 1, 2, 3), ((0,), (2,), (1, 3)), table, raw_traces, channel_mask)
    from_core = swap(leaving13, 0, 1)
    own1 = from_core[:rows]
    same = jnp.concatenate([own0, own1])
    cross = jnp.concatenate([leaving2, from_core[rows:]])
    far01 = swap(same, far, 0)
    far23 = swap(cross, far, 2)
    arrived = swap(cross, 0, 2)
    own2, own3 = arrived[:rows], arrived[rows:]
    own0_next, arrived = tie(own0, arrived)
    near0, near1 = swap_blk(own0_next, 1), swap_blk(own1, 1)
    near2, near3 = swap_blk(own2, 1), swap_blk(own3, 1)
    near = [(near0, 0), (near1, 0), (near2, 0), (near3, 0)]
    own = [(same, 0), (same, -BAND), (arrived, 0), (arrived, -BAND)]
    second, left = cross_blocks(own, near, 0, BAND)
    far01, far23, second = tie(far01, far23, second)
    far_pieces = [(far01, 0), (far01, -BAND), (far23, 0), (far23, -BAND)]
    (first,) = cross_blocks(own, far_pieces, 0, BAND, left)
    return first, second


def solution(mesh):
    in_specs = (P("win", None, "blk"), P("win", "blk"))
    out_specs = (P("win", None, "blk", None), P("win", None, "blk", None))
    return jax.shard_map(body, mesh=mesh, in_specs=in_specs, out_specs=out_specs, check_vma=False)
```
